128 devices in a mesh: dp: 128 (over x, y, z, core).
Axes of the slice: x: 4, y: 4, z: 4, core: 2. Of those that a mesh axis runs over, the one named last changes fastest.
Arguments:
- images: float32 [81920, 1152], P('dp'), may hold values from -0.4375 to 0.4375
- texts: float32 [81920, 1152], P('dp'), may hold values from -0.4375 to 0.4375
- log_scale: float32 [1], replicated, may hold values from 3.9 to 4.8
- bias: float32 [1], replicated, may hold values from -3 to 0
Outputs:
- image_grad: float32 [81920, 1152], P('dp')
- text_grad: float32 [81920, 1152], P('dp')
The draws below stay inside these ranges and needn't reach their ends.
All inputs are finite; a program needn't handle non-finite values.
Results may differ from the reference program's by a relative error of at most 0.00011.
Values sent between devices are 32-bit elements; how exact they have to be, the bound alone decides.
No kernel may reach another device: no remote copies, remote signals or barrier semaphores. Data moves between devices by JAX's collectives and lax.ppermute only.
A program may use at most 128 MiB of HBM per device.

```python
import jax
import jax.numpy as jnp
from jax import lax

D = 1152
ROWS_DEV = 640
STEPS = 2
BATCH = 81920
N_DP = 128


def level_of(key, shape, pieces, low, top_value):
    gain, own = 1.0, jax.random.fold_in(key, 6)
    for axis_at, shards_of in pieces:
        steps = jnp.exp(jax.random.uniform(jax.random.fold_in(own, axis_at), (shards_of,), jnp.float32, low / len(pieces), top_value / len(pieces)))
        gain = gain * jnp.repeat(steps, shape[axis_at] // shards_of).reshape([-1 if axis == axis_at else 1 for axis in range(len(shape))])
    return gain


def normal_values(own_key, dims, spread, most, shards=(), kind=jnp.bfloat16):
    array = spread * jax.random.normal(own_key, dims, jnp.float32)
    if shards:
        array = array * level_of(own_key, dims, shards, -0.22, 0.18)
    return jnp.clip(array, -most, most).astype(kind)


def setup_inputs(seed: int = 0) -> dict:
    key_list = jax.random.split(jax.random.key(seed), 5)
    return {
        "images": normal_values(key_list[0], (BATCH, D), 0.03, 0.4375, ((0, 128),), jnp.float32),
        "texts": normal_values(key_list[1], (BATCH, D), 0.03, 0.4375, ((0, 128),), jnp.float32),
        "log_scale": jnp.clip(jax.random.uniform(key_list[2], (1,), jnp.float32, 3.9, 4.8), 3.9, 4.8),
        "bias": jnp.clip(jax.random.uniform(key_list[3], (1,), jnp.float32, -3.0, 0.0), -3.0, 0.0),
    }


EPSILON = 1e-06

def unit_rows(values):
    norms = jnp.sqrt(lax.optimization_barrier(jnp.sum(values * values, axis=-1, keepdims=True)) + EPSILON)
    return (values / norms, norms)

def tangent(unit, grad, norms):
    return (grad - unit * lax.optimization_barrier(jnp.sum(unit * grad, axis=-1, keepdims=True))) / norms

def reference(images, texts, log_scale, bias):
    scale = jnp.exp(log_scale[0])
    bias_value = bias[0]
    image_unit, image_norm = unit_rows(images.reshape(N_DP, ROWS_DEV, D))
    text_unit, text_norm = unit_rows(texts.reshape(N_DP, ROWS_DEV, D))
    image_acc = jnp.zeros((N_DP, ROWS_DEV, D), jnp.float32)
    text_acc = jnp.zeros((N_DP, ROWS_DEV, D), jnp.float32)
    for offset in range(-STEPS, STEPS + 1):
        partner = jnp.roll(text_unit, -offset, axis=0)
        logits = scale * jnp.einsum('krd,kcd->krc', image_unit, partner, precision=lax.Precision.HIGHEST) + bias_value
        if offset == 0:
            labels = 2.0 * jnp.eye(ROWS_DEV, dtype=jnp.float32) - 1.0
        else:
            labels = -jnp.ones((ROWS_DEV, ROWS_DEV), jnp.float32)
        slopes = -labels * jax.nn.sigmoid(-labels * logits) / ROWS_DEV
        image_acc = image_acc + scale * jnp.einsum('krc,kcd->krd', slopes, partner, precision=lax.Precision.HIGHEST)
        terms = scale * jnp.einsum('krc,krd->kcd', slopes, image_unit, precision=lax.Precision.HIGHEST)
        text_acc = text_acc + jnp.roll(terms, offset, axis=0)
    image_grad = tangent(image_unit, image_acc, image_norm).reshape(BATCH, D)
    text_grad = tangent(text_unit, text_acc, text_norm).reshape(BATCH, D)
    return (image_grad, text_grad)
```

```python
import jax
import jax.numpy as jnp
from jax import lax
from jax.sharding import PartitionSpec as P

EPSILON = 1e-06
PRECISION = lax.Precision.HIGH


def unit_rows(values):
    norms = jnp.sqrt(jnp.sum(values * values, axis=-1, keepdims=True) + EPSILON)
    return (values / norms, norms)


def tangent(unit, grad, norms):
    return (grad - unit * jnp.sum(unit * grad, axis=-1, keepdims=True)) / norms


def dot(a, b, da, db):
    return lax.dot_general(a, b, (((da,), (db,)), ((), ())), precision=PRECISION)


def on_device(images, texts, log_scale, bias):
    n = lax.axis_size("dp")
    rows = images.shape[0]
    wide = [((i + 2) % n if i % 2 == 0 else (i - 2) % n, i) for i in range(n)]
    narrow = [((i - 2) % n if i % 2 == 0 else (i + 2) % n, i) for i in range(n)]
    swap = [(i ^ 1, i) for i in range(n)]
    wide_back = [(b, a) for a, b in wide]
    narrow_back = [(b, a) for a, b in narrow]

    wide_texts = lax.ppermute(texts, "dp", wide)
    other_images = lax.ppermute(images, "dp", swap)

    scale = jnp.exp(log_scale[0])
    bias_value = bias[0]
    image_unit, image_norm = unit_rows(images)
    other_unit, _ = unit_rows(other_images)
    text_unit, text_norm = unit_rows(texts)
    both = jnp.concatenate([image_unit, other_unit], axis=0)

    def slopes(image_rows, text_rows):
        logits = scale * dot(image_rows, text_rows, 1, 1) + bias_value
        return jax.nn.sigmoid(logits) / rows

    logits = scale * dot(both, text_unit, 1, 1) + bias_value
    r = lax.broadcasted_iota(jnp.int32, logits.shape, 0)
    c = lax.broadcasted_iota(jnp.int32, logits.shape, 1)
    label = jnp.where(r == c, 1.0, -1.0)
    s = -label * jax.nn.sigmoid(-label * logits) / rows
    both_acc = dot(s, text_unit, 1, 0)
    text_acc = dot(s, both, 0, 0)

    wide_texts, texts_later = lax.optimization_barrier((wide_texts, texts))
    narrow_texts = lax.ppermute(texts_later, "dp", narrow)

    unit, _ = unit_rows(wide_texts)
    s = slopes(both, unit)
    wide_grad = lax.ppermute(scale * dot(s, both, 0, 0), "dp", wide_back)
    both_acc = both_acc + dot(s, unit, 1, 0)
    other_acc = lax.ppermute(both_acc[rows:], "dp", swap)

    unit, _ = unit_rows(narrow_texts)
    s = slopes(image_unit, unit)
    narrow_grad = lax.ppermute(scale * dot(s, image_unit, 0, 0), "dp", narrow_back)
    image_acc = scale * (both_acc[:rows] + dot(s, unit, 1, 0) + other_acc)
    image_grad = tangent(image_unit, image_acc, image_norm)

    text_acc = scale * text_acc + wide_grad + narrow_grad
    text_grad = tangent(text_unit, text_acc, text_norm)
    return (image_grad, text_grad)


def solution(mesh):
    in_specs = (P("dp", None), P("dp", None), P(), P())
    out_specs = (P("dp", None), P("dp", None))
    return jax.shard_map(
        on_device, mesh=mesh, in_specs=in_specs, out_specs=out_specs, check_vma=False
    )
```

```python
import functools

import jax
import jax.numpy as jnp
from jax import lax
from jax.experimental import pallas as pl
from jax.experimental.pallas import tpu as pltpu
from jax.sharding import PartitionSpec as P

EPSILON = 1e-06
TILE = 320
FIRST = 384
MIB = 1024 * 1024
F32 = jnp.float32
BF16 = jnp.bfloat16


def split(values):
    high = values.astype(BF16)
    return high, (values - high.astype(F32)).astype(BF16)


def inverse_norm(values):
    return lax.rsqrt(jnp.sum(values * values, axis=-1, keepdims=True) + EPSILON)


def product(a_high, a_low, b_high, b_low, a_dim, b_dim):
    dims = (((a_dim,), (b_dim,)), ((), ()))
    dot = functools.partial(lax.dot_general, dimension_numbers=dims, preferred_element_type=F32)
    return dot(a_high, b_high) + (dot(a_high, b_low) + dot(a_low, b_high))


def split_rows(source, high, low, at=0):
    step = 128

    @pl.loop(0, source.shape[0] // step)
    def _(i):
        values = source[pl.ds(pl.multiple_of(i * step, step), step), :]
        out = pl.ds(pl.multiple_of(at + i * step, step), step)
        high[out, :], low[out, :] = split(values * inverse_norm(values))


def slope_rows(numbers, at, count, image_high, image_low, text_high, text_low, logits, slope_high, slope_low, diagonal=False):
    scale, bias, gain = numbers[0], numbers[1], numbers[2]
    step = 64
    rows = pl.ds(at, count)
    logits[pl.ds(0, count), :] = product(text_high[rows, :], text_low[rows, :], image_high[...], image_low[...], 1, 1)

    @pl.loop(0, count // step)
    def _(k):
        x = scale * logits[pl.ds(pl.multiple_of(k * step, step), step), :] + bias
        start = pl.multiple_of(at + k * step, step)
        if diagonal:
            j = lax.broadcasted_iota(jnp.int32, x.shape, 0) + start
            i = lax.broadcasted_iota(jnp.int32, x.shape, 1)
            sign = jnp.where(i == j, -1.0, 1.0)
            slopes = (gain * sign) / (1.0 + jnp.exp(-sign * x))
        else:
            slopes = gain / (1.0 + jnp.exp(-x))
        out = pl.ds(start, step)
        slope_high[out, :], slope_low[out, :] = split(slopes)

    return product(slope_high[rows, :], slope_low[rows, :], image_high[...], image_low[...], 1, 0)


def image_tiles(rows):
    return [(at, min(256, rows - at)) for at in range(0, rows, 256)]


def image_sum(slope_high, slope_low, text_high, text_low, at, count):
    columns = pl.ds(at, count)
    return product(slope_high[:, columns], slope_low[:, columns], text_high[...], text_low[...], 0, 0)


def tangent_of(values, grad):
    inverse = inverse_norm(values)
    unit = values * inverse
    return (grad - unit * jnp.sum(unit * grad, axis=-1, keepdims=True)) * inverse


def own_kernel(numbers, images, others, texts, both_high, both_low, text_acc, image_acc, other_acc, text_high, text_low, logits, slope_high, slope_low):
    rows = texts.shape[0]
    split_rows(images, both_high, both_low)
    split_rows(others, both_high, both_low, rows)
    split_rows(texts, text_high, text_low)
    for at in range(0, rows, TILE):
        text_acc[pl.ds(at, TILE), :] = slope_rows(
            numbers, at, TILE, both_high, both_low, text_high, text_low, logits, slope_high, slope_low, True
        )
    for at, count in image_tiles(rows):
        image_acc[pl.ds(at, count), :] = image_sum(slope_high, slope_low, text_high, text_low, at, count)
        other_acc[pl.ds(at, count), :] = image_sum(slope_high, slope_low, text_high, text_low, rows + at, count)


def wide_kernel(numbers, image_high, image_low, texts, known, grad, other_acc, slope_high, slope_low, text_high, text_low, logits):
    rows = texts.shape[0]
    split_rows(texts, text_high, text_low)
    for at in range(0, rows, TILE):
        grad[pl.ds(at, TILE), :] = slope_rows(
            numbers, at, TILE, image_high, image_low, text_high, text_low, logits, slope_high, slope_low
        )
    for at, count in image_tiles(rows):
        place = pl.ds(at, count)
        other_acc[place, :] = known[place, :] + image_sum(slope_high, slope_low, text_high, text_low, rows + at, count)


def narrow_kernel(numbers, both_high, both_low, texts, first, second, slope_high, slope_low, text_high, text_low, logits):
    rows = texts.shape[0]
    split_rows(texts, text_high, text_low)
    image_high, image_low = both_high.at[pl.ds(0, rows)], both_low.at[pl.ds(0, rows)]
    at = 0
    for out in (first, second):
        count = out.shape[0]
        out[...] = slope_rows(
            numbers, at, count, image_high, image_low, text_high, text_low, logits, slope_high, slope_low
        )
        at += count


def image_kernel(w0, w1, w2, w3, n0, n1, n2, n3, images, known, received, out):
    for at, count in image_tiles(out.shape[0]):
        rows = pl.ds(at, count)
        grad = image_sum(w0, w1, w2, w3, at, count) + image_sum(n0, n1, n2, n3, at, count)
        out[rows, :] = grad + known[rows, :] + received[rows, :]
    step = 64

    @pl.loop(0, out.shape[0] // step)
    def _(k):
        rows = pl.ds(pl.multiple_of(k * step, step), step)
        out[rows, :] = tangent_of(images[rows, :], out[rows, :])


def text_kernel(first, texts, known, wide, narrow, *refs):
    out, tangents, arrived = refs[-3:]
    step = 64
    copies = []
    for at in range(0, narrow.shape[0], step):
        here, there = pl.ds(at, step), pl.ds(first + at, step)
        grad = known[there, :] + wide[there, :] + narrow[here, :]
        tangents[here, :] = tangent_of(texts[there, :], grad)
        copies.append(pltpu.make_async_copy(tangents.at[here], out.at[there], arrived.at[at // step]))
        copies[-1].start()
    for copy in copies:
        copy.wait()


def cost(units):
    return pl.CostEstimate(flops=int(units * 6 * 640 * 640 * 1152), bytes_accessed=5_000_000, transcendentals=0)


IN_SMEM = pl.BlockSpec(memory_space=pltpu.SMEM)
IN_VMEM = pl.BlockSpec(memory_space=pltpu.VMEM)


def near(value):
    return pltpu.with_memory_space_constraint(value, pltpu.VMEM)


def vmem_call(kernel, outs, scratch, units, *arrays, numbers=None):
    scalars = () if numbers is None else (numbers,)
    return pl.pallas_call(
        kernel,
        out_shape=[pltpu.VMEM(shape, kind) for shape, kind in outs],
        in_specs=[IN_SMEM] * len(scalars) + [IN_VMEM] * len(arrays),
        out_specs=[IN_VMEM] * len(outs),
        scratch_shapes=[pltpu.VMEM(shape, kind) for shape, kind in scratch],
        compiler_params=pltpu.CompilerParams(vmem_limit_bytes=20 * MIB),
        cost_estimate=cost(units),
    )(*scalars, *(near(a) for a in arrays))


def finish_rows(first, texts, known, wide, narrow, out=None):
    before = () if out is None else (out,)
    return pl.pallas_call(
        functools.partial(text_kernel, first),
        out_shape=jax.ShapeDtypeStruct(texts.shape, F32),
        in_specs=[IN_VMEM] * 4 + [pl.BlockSpec(memory_space=pl.ANY)] * len(before),
        out_specs=pl.BlockSpec(memory_space=pl.ANY),
        scratch_shapes=[pltpu.VMEM(narrow.shape, F32), pltpu.SemaphoreType.DMA((narrow.shape[0] // 64,))],
        input_output_aliases={4: 0} if before else {},
        compiler_params=pltpu.CompilerParams(vmem_limit_bytes=8 * MIB),
        cost_estimate=cost(0),
    )(near(texts), near(known), near(wide), near(narrow), *before)


def on_device(images, texts, log_scale, bias):
    n = lax.axis_size("dp")
    rows, width = images.shape
    wide = [((i + 2) % n if i % 2 == 0 else (i - 2) % n, i) for i in range(n)]
    narrow = [((i - 2) % n if i % 2 == 0 else (i + 2) % n, i) for i in range(n)]
    swap = [(i ^ 1, i) for i in range(n)]
    wide_back = [(b, a) for a, b in wide]
    narrow_back = [(b, a) for a, b in narrow]
    block, half = ((rows, width), F32), ((rows, width), BF16)
    both = ((2 * rows, width), BF16)
    slopes_wide, slopes_narrow = ((rows, 2 * rows), BF16), ((rows, rows), BF16)

    wide_texts = lax.ppermute(texts, "dp", wide)
    others = lax.ppermute(images, "dp", swap)
    scale = jnp.exp(log_scale)
    numbers = jnp.concatenate([scale, bias, scale / rows])

    both_high, both_low, text_acc, image_acc, other_acc = vmem_call(
        own_kernel,
        [both, both, block, block, block],
        [half, half, ((TILE, 2 * rows), F32), slopes_wide, slopes_wide],
        6,
        images,
        others,
        texts,
        numbers=numbers,
    )

    other_acc, texts_later, both_high = lax.optimization_barrier((other_acc, texts, both_high))
    narrow_texts = lax.ppermute(texts_later, "dp", narrow)

    wide_grad, other_acc, *wide_quad = vmem_call(
        wide_kernel,
        [block, block, slopes_wide, slopes_wide, half, half],
        [((TILE, 2 * rows), F32)],
        5,
        both_high,
        both_low,
        wide_texts,
        other_acc,
        numbers=numbers,
    )
    wide_grad = lax.ppermute(wide_grad, "dp", wide_back)
    received = lax.ppermute(other_acc, "dp", swap)

    first, second, *narrow_quad = vmem_call(
        narrow_kernel,
        [((FIRST, width), F32), ((rows - FIRST, width), F32), slopes_narrow, slopes_narrow, half, half],
        [((FIRST, rows), F32)],
        2,
        both_high,
        both_low,
        narrow_texts,
        numbers=numbers,
    )
    first = lax.ppermute(first, "dp", narrow_back)
    second = lax.ppermute(second, "dp", narrow_back)

    (image_grad,) = vmem_call(
        image_kernel, [block], [], 2, *wide_quad, *narrow_quad, images, image_acc, received
    )
    text_grad = finish_rows(0, texts, text_acc, wide_grad, first)
    text_grad = finish_rows(FIRST, texts, text_acc, wide_grad, second, text_grad)
    return (image_grad, text_grad)


def solution(mesh):
    in_specs = (P("dp", None), P("dp", None), P(), P())
    out_specs = (P("dp", None), P("dp", None))
    return jax.shard_map(
        on_device, mesh=mesh, in_specs=in_specs, out_specs=out_specs, check_vma=False
    )
```

```python
import functools

import jax
import jax.numpy as jnp
from jax import lax
from jax.experimental import pallas as pl
from jax.experimental.pallas import tpu as pltpu
from jax.sharding import PartitionSpec as P

EPSILON = 1e-06
TILE = 320
FIRST = 384
MIB = 1024 * 1024
F32 = jnp.float32
BF16 = jnp.bfloat16


def split(values):
    high = values.astype(BF16)
    return high, (values - high.astype(F32)).astype(BF16)


def inverse_norm(values):
    return lax.rsqrt(jnp.sum(values * values, axis=-1, keepdims=True) + EPSILON)


def product(a_high, a_low, b_high, b_low, a_dim, b_dim):
    dims = (((a_dim,), (b_dim,)), ((), ()))
    dot = functools.partial(lax.dot_general, dimension_numbers=dims, preferred_element_type=F32)
    return dot(a_high, b_high) + (dot(a_high, b_low) + dot(a_low, b_high))


def split_rows(source, high, low, at=0):
    step = 128

    @pl.loop(0, source.shape[0] // step)
    def _(i):
        values = source[pl.ds(pl.multiple_of(i * step, step), step), :]
        out = pl.ds(pl.multiple_of(at + i * step, step), step)
        high[out, :], low[out, :] = split(values * inverse_norm(values))


def logit_rows(at, count, image_high, image_low, text_high, text_low, logits):
    rows = pl.ds(at, count)
    logits[rows, :] = product(text_high[rows, :], text_low[rows, :], image_high[...], image_low[...], 1, 1)


def slope_rows(numbers, at, count, logits, slope_high, slope_low, diagonal=False):
    log_scale, bias = numbers
    scale = jnp.exp(jnp.full((1, logits.shape[1]), log_scale[0], F32))
    gain = scale * (1.0 / logits.shape[0])
    step = 64

    @pl.loop(0, count // step)
    def _(k):
        start = pl.multiple_of(at + k * step, step)
        rows = pl.ds(start, step)
        x = scale * logits[rows, :] + bias[0]
        if diagonal:
            j = lax.broadcasted_iota(jnp.int32, x.shape, 0) + start
            i = lax.broadcasted_iota(jnp.int32, x.shape, 1)
            sign = jnp.where(i == j, -1.0, 1.0)
            slopes = (gain * sign) / (1.0 + jnp.exp(-sign * x))
        else:
            slopes = gain / (1.0 + jnp.exp(-x))
        slope_high[rows, :], slope_low[rows, :] = split(slopes)


def text_sum(at, count, slope_high, slope_low, image_high, image_low):
    rows = pl.ds(at, count)
    return product(slope_high[rows, :], slope_low[rows, :], image_high[...], image_low[...], 1, 0)


def text_side(numbers, image_high, image_low, text_high, text_low, logits, slope_high, slope_low, grads, diagonal=False):
    rows = text_high.shape[0]
    for at in range(0, rows, TILE):
        logit_rows(at, TILE, image_high, image_low, text_high, text_low, logits)
    slope_rows(numbers, 0, rows, logits, slope_high, slope_low, diagonal)
    first = 0
    for grad in grads:
        count = grad.shape[0]
        for at in range(0, count, TILE if count == rows else count):
            size = min(TILE, count) if count == rows else count
            grad[pl.ds(at, size), :] = text_sum(first + at, size, slope_high, slope_low, image_high, image_low)
        first += count


def image_tiles(rows):
    return [(at, min(256, rows - at)) for at in range(0, rows, 256)]


def image_sum(slope_high, slope_low, text_high, text_low, at, count):
    columns = pl.ds(at, count)
    return product(slope_high[:, columns], slope_low[:, columns], text_high[...], text_low[...], 0, 0)


def tangent_of(values, grad):
    inverse = inverse_norm(values)
    unit = values * inverse
    return (grad - unit * jnp.sum(unit * grad, axis=-1, keepdims=True)) * inverse


def prepare_kernel(images, texts, both_high, both_low, text_high, text_low, kept, own, arrived):
    step = 128
    parts = images.shape[0] // step
    copies = []
    for k in range(parts):
        rows = pl.ds(k * step, step)
        copies.append(pltpu.make_async_copy(images.at[rows], own.at[rows], arrived.at[k]))
    for k in range(parts):
        rows = pl.ds(k * step, step)
        copies.append(pltpu.make_async_copy(texts.at[rows], kept.at[rows], arrived.at[parts + k]))
    for copy in copies:
        copy.start()
    for k, copy in enumerate(copies):
        copy.wait()
        source, high, low = (own, both_high, both_low) if k < parts else (kept, text_high, text_low)
        rows = pl.ds(k % parts * step, step)
        values = source[rows, :]
        high[rows, :], low[rows, :] = split(values * inverse_norm(values))


def own_kernel(log_scale, bias, others, text_high, text_low, high_in, low_in, both_high, both_low, text_acc, image_acc, slope_high, slope_low, logits):
    rows = others.shape[0]
    split_rows(others, both_high, both_low, rows)
    numbers = log_scale, bias
    text_side(numbers, both_high, both_low, text_high, text_low, logits, slope_high, slope_low, [text_acc], True)
    for at, count in image_tiles(rows):
        image_acc[pl.ds(at, count), :] = image_sum(slope_high, slope_low, text_high, text_low, at, count)


def wide_kernel(log_scale, bias, image_high, image_low, texts, grad, slope_high, slope_low, text_high, text_low, logits):
    split_rows(texts, text_high, text_low)
    numbers = log_scale, bias
    text_side(numbers, image_high, image_low, text_high, text_low, logits, slope_high, slope_low, [grad])


def narrow_kernel(log_scale, bias, both_high, both_low, texts, known, w0, w1, w2, w3, first, second, image_acc, slope_high, slope_low, text_high, text_low, logits):
    rows = texts.shape[0]
    split_rows(texts, text_high, text_low)
    image_high, image_low = both_high.at[pl.ds(0, rows)], both_low.at[pl.ds(0, rows)]
    numbers = log_scale, bias
    text_side(numbers, image_high, image_low, text_high, text_low, logits, slope_high, slope_low, [first, second])
    for at, count in image_tiles(rows):
        place = pl.ds(at, count)
        grad = image_sum(w0, w1, w2, w3, at, count)
        grad = grad + image_sum(slope_high, slope_low, text_high, text_low, at, count)
        image_acc[place, :] = known[place, :] + grad


def other_kernel(o0, o1, o2, o3, w0, w1, w2, w3, out):
    rows = out.shape[0]
    for at, count in image_tiles(rows):
        total = image_sum(o0, o1, o2, o3, rows + at, count) + image_sum(w0, w1, w2, w3, rows + at, count)
        out[pl.ds(at, count), :] = total


def image_kernel(images, known, received, out):
    out[...] = tangent_of(images[...], known[...] + received[...])


def add_kernel(left, right, out):
    out[...] = left[...] + right[...]


def text_kernel(first, texts, known, narrow, *refs):
    out, tangents, arrived = refs[-3:]
    step = 64
    copies = []
    for at in range(0, narrow.shape[0], step):
        here, there = pl.ds(at, step), pl.ds(first + at, step)
        grad = known[there, :] + narrow[here, :]
        tangents[here, :] = tangent_of(texts[there, :], grad)
        copies.append(pltpu.make_async_copy(tangents.at[here], out.at[there], arrived.at[at // step]))
        copies[-1].start()
    for copy in copies:
        copy.wait()


def cost(units):
    flops = int(units * 6 * 640 * 640 * 1152)
    return pl.CostEstimate(flops=flops, bytes_accessed=5_000_000 if units else 0, transcendentals=0)


IN_SMEM = pl.BlockSpec(memory_space=pltpu.SMEM)
IN_VMEM = pl.BlockSpec(memory_space=pltpu.VMEM)


def near(value):
    return pltpu.with_memory_space_constraint(value, pltpu.VMEM)


def vmem_call(kernel, outs, scratch, units, *arrays, numbers=(), aliases=None, limit=8, space=pltpu.VMEM):
    return pl.pallas_call(
        kernel,
        out_shape=[pltpu.VMEM(shape, kind) for shape, kind in outs],
        in_specs=[IN_SMEM] * len(numbers) + [pl.BlockSpec(memory_space=space)] * len(arrays),
        out_specs=[IN_VMEM] * len(outs),
        scratch_shapes=scratch,
        input_output_aliases=aliases or {},
        compiler_params=pltpu.CompilerParams(vmem_limit_bytes=limit * MIB),
        cost_estimate=cost(units),
    )(*numbers, *(pltpu.with_memory_space_constraint(a, space) for a in arrays))


def finish_images(images, known, received):
    rows, width = images.shape
    block = pl.BlockSpec((128, width), lambda i: (i, 0))
    return pl.pallas_call(
        image_kernel,
        grid=(rows // 128,),
        out_shape=jax.ShapeDtypeStruct(images.shape, F32),
        in_specs=[block] * 3,
        out_specs=block,
        compiler_params=pltpu.CompilerParams(vmem_limit_bytes=8 * MIB),
        cost_estimate=cost(0),
    )(images, known, received)


def finish_rows(first, texts, known, narrow, out=None):
    before = () if out is None else (out,)
    return pl.pallas_call(
        functools.partial(text_kernel, first),
        out_shape=jax.ShapeDtypeStruct(texts.shape, F32),
        in_specs=[IN_VMEM] * 3 + [pl.BlockSpec(memory_space=pl.ANY)] * len(before),
        out_specs=pl.BlockSpec(memory_space=pl.ANY),
        scratch_shapes=[pltpu.VMEM(narrow.shape, F32), pltpu.SemaphoreType.DMA((narrow.shape[0] // 64,))],
        input_output_aliases={3: 0} if before else {},
        compiler_params=pltpu.CompilerParams(vmem_limit_bytes=8 * MIB),
        cost_estimate=cost(0),
    )(near(texts), near(known), near(narrow), *before)


def on_device(images, texts, log_scale, bias):
    n = lax.axis_size("dp")
    rows, width = images.shape
    wide = [((i + 2) % n if i % 2 == 0 else (i - 2) % n, i) for i in range(n)]
    narrow = [((i - 2) % n if i % 2 == 0 else (i + 2) % n, i) for i in range(n)]
    swap = [(i ^ 1, i) for i in range(n)]
    wide_back = [(b, a) for a, b in wide]
    narrow_back = [(b, a) for a, b in narrow]
    block, half = ((rows, width), F32), ((rows, width), BF16)
    both = ((2 * rows, width), BF16)
    logits_wide, logits_narrow = pltpu.VMEM((rows, 2 * rows), F32), pltpu.VMEM((rows, rows), F32)
    slopes_wide, slopes_narrow = ((rows, 2 * rows), BF16), ((rows, rows), BF16)
    numbers = log_scale, bias

    wide_texts = lax.ppermute(texts, "dp", wide)
    others = lax.ppermute(images, "dp", swap)

    both_high, both_low, text_high, text_low, kept = vmem_call(
        prepare_kernel,
        [both, both, half, half, block],
        [pltpu.VMEM((rows, width), F32), pltpu.SemaphoreType.DMA((2 * rows // 128,))],
        0,
        images,
        texts,
        space=pltpu.HBM,
    )
    both_high, both_low, text_acc, image_acc, *own_slopes = vmem_call(
        own_kernel,
        [both, both, block, block, slopes_wide, slopes_wide],
        [logits_wide],
        5,
        others,
        text_high,
        text_low,
        both_high,
        both_low,
        numbers=numbers,
        aliases={5: 0, 6: 1},
    )

    image_acc, kept, both_high = lax.optimization_barrier((image_acc, kept, both_high))
    narrow_texts = lax.ppermute(kept, "dp", narrow)

    wide_grad, *wide_quad = vmem_call(
        wide_kernel,
        [block, slopes_wide, slopes_wide, half, half],
        [logits_wide],
        4,
        both_high,
        both_low,
        wide_texts,
        numbers=numbers,
    )
    wide_grad = lax.ppermute(wide_grad, "dp", wide_back)

    (other_acc,) = vmem_call(other_kernel, [block], [], 0, *own_slopes, text_high, text_low, *wide_quad)
    first, second, image_acc = vmem_call(
        narrow_kernel,
        [((FIRST, width), F32), ((rows - FIRST, width), F32), block],
        [pltpu.VMEM(*slopes_narrow)] * 2 + [pltpu.VMEM(*half)] * 2 + [logits_narrow],
        4,
        both_high,
        both_low,
        narrow_texts,
        image_acc,
        *wide_quad,
        numbers=numbers,
        aliases={5: 2},
        limit=10,
    )
    first = lax.ppermute(first, "dp", narrow_back)
    second = lax.ppermute(second, "dp", narrow_back)
    received = lax.ppermute(other_acc, "dp", swap)

    (known,) = vmem_call(add_kernel, [block], [], 6, text_acc, wide_grad, aliases={0: 0})
    image_acc, known = lax.optimization_barrier((image_acc, known))
    image_grad = finish_images(images, image_acc, received)
    image_grad, known = lax.optimization_barrier((image_grad, known))
    text_grad = finish_rows(0, kept, known, first)
    text_grad = finish_rows(FIRST, kept, known, second, text_grad)
    return (image_grad, text_grad)


def solution(mesh):
    in_specs = (P("dp", None), P("dp", None), P(), P())
    out_specs = (P("dp", None), P("dp", None))
    return jax.shard_map(
        on_device, mesh=mesh, in_specs=in_specs, out_specs=out_specs, check_vma=False
    )
```

```python
import functools

import jax
import jax.numpy as jnp
from jax import lax
from jax.experimental import pallas as pl
from jax.experimental.pallas import tpu as pltpu
from jax.sharding import PartitionSpec as P

EPSILON = 1e-06
TILE = 320
FIRST = 512
EARLY = 256
MIB = 1024 * 1024
F32 = jnp.float32
BF16 = jnp.bfloat16


def split(values):
    high = values.astype(BF16)
    return high, (values - high.astype(F32)).astype(BF16)


def inverse_norm(values):
    return lax.rsqrt(jnp.sum(values * values, axis=-1, keepdims=True) + EPSILON)


def product(a_high, a_low, b_high, b_low, a_dim, b_dim):
    dims = (((a_dim,), (b_dim,)), ((), ()))
    dot = functools.partial(lax.dot_general, dimension_numbers=dims, preferred_element_type=F32)
    return dot(a_high, b_high) + (dot(a_high, b_low) + dot(a_low, b_high))


def split_rows(source, high, low, at=0):
    step = 128

    @pl.loop(0, source.shape[0] // step)
    def _(i):
        values = source[pl.ds(pl.multiple_of(i * step, step), step), :]
        out = pl.ds(pl.multiple_of(at + i * step, step), step)
        high[out, :], low[out, :] = split(values * inverse_norm(values))


def logit_rows(at, count, image_high, image_low, text_high, text_low, logits):
    rows = pl.ds(at, count)
    logits[rows, :] = product(text_high[rows, :], text_low[rows, :], image_high[...], image_low[...], 1, 1)


def slope_rows(numbers, at, count, logits, slope_high, slope_low, diagonal=False):
    log_scale, bias = numbers
    scale = jnp.exp(jnp.full((1, logits.shape[1]), log_scale[0], F32))
    gain = scale * (1.0 / logits.shape[0])
    step = 64

    @pl.loop(0, count // step)
    def _(k):
        start = pl.multiple_of(at + k * step, step)
        rows = pl.ds(start, step)
        x = scale * logits[rows, :] + bias[0]
        if diagonal:
            j = lax.broadcasted_iota(jnp.int32, x.shape, 0) + start
            i = lax.broadcasted_iota(jnp.int32, x.shape, 1)
            sign = jnp.where(i == j, -1.0, 1.0)
            slopes = (gain * sign) / (1.0 + jnp.exp(-sign * x))
        else:
            slopes = gain / (1.0 + jnp.exp(-x))
        slope_high[rows, :], slope_low[rows, :] = split(slopes)


def text_sum(at, count, slope_high, slope_low, image_high, image_low):
    rows = pl.ds(at, count)
    return product(slope_high[rows, :], slope_low[rows, :], image_high[...], image_low[...], 1, 0)


def text_side(numbers, image_high, image_low, text_high, text_low, logits, slope_high, slope_low, grads, diagonal=False):
    rows = text_high.shape[0]
    for at in range(0, rows, TILE):
        logit_rows(at, TILE, image_high, image_low, text_high, text_low, logits)
    slope_rows(numbers, 0, rows, logits, slope_high, slope_low, diagonal)
    first = 0
    for grad in grads:
        count = grad.shape[0]
        for at in range(0, count, TILE if count == rows else count):
            size = min(TILE, count) if count == rows else count
            grad[pl.ds(at, size), :] = text_sum(first + at, size, slope_high, slope_low, image_high, image_low)
        first += count


def image_tiles(rows):
    return [(at, min(256, rows - at)) for at in range(0, rows, 256)]


def image_sum(slope_high, slope_low, text_high, text_low, at, count):
    columns = pl.ds(at, count)
    return product(slope_high[:, columns], slope_low[:, columns], text_high[...], text_low[...], 0, 0)


def tangent_of(values, grad):
    inverse = inverse_norm(values)
    unit = values * inverse
    return (grad - unit * jnp.sum(unit * grad, axis=-1, keepdims=True)) * inverse


def prepare_kernel(images, texts, both_high, both_low, text_high, text_low, kept, own, arrived):
    step = 128
    parts = images.shape[0] // step
    copies = []
    for k in range(parts):
        rows = pl.ds(k * step, step)
        copies.append(pltpu.make_async_copy(images.at[rows], own.at[rows], arrived.at[k]))
    for k in range(parts):
        rows = pl.ds(k * step, step)
        copies.append(pltpu.make_async_copy(texts.at[rows], kept.at[rows], arrived.at[parts + k]))
    for copy in copies:
        copy.start()
    for k, copy in enumerate(copies):
        copy.wait()
        source, high, low = (own, both_high, both_low) if k < parts else (kept, text_high, text_low)
        rows = pl.ds(k % parts * step, step)
        values = source[rows, :]
        high[rows, :], low[rows, :] = split(values * inverse_norm(values))


def own_kernel(log_scale, bias, others, text_high, text_low, high_in, low_in, both_high, both_low, text_acc, image_acc, slope_high, slope_low, logits):
    rows = others.shape[0]
    split_rows(others, both_high, both_low, rows)
    numbers = log_scale, bias
    text_side(numbers, both_high, both_low, text_high, text_low, logits, slope_high, slope_low, [text_acc], True)
    for at, count in image_tiles(image_acc.shape[0]):
        image_acc[pl.ds(at, count), :] = image_sum(slope_high, slope_low, text_high, text_low, at, count)


def wide_kernel(log_scale, bias, image_high, image_low, texts, grad, slope_high, slope_low, text_high, text_low, logits):
    split_rows(texts, text_high, text_low)
    numbers = log_scale, bias
    text_side(numbers, image_high, image_low, text_high, text_low, logits, slope_high, slope_low, [grad])


def narrow_kernel(log_scale, bias, both_high, both_low, texts, known, o0, o1, o2, o3, w0, w1, w2, w3, first, second, image_acc, slope_high, slope_low, text_high, text_low, logits):
    rows = texts.shape[0]
    split_rows(texts, text_high, text_low)
    image_high, image_low = both_high.at[pl.ds(0, rows)], both_low.at[pl.ds(0, rows)]
    numbers = log_scale, bias
    text_side(numbers, image_high, image_low, text_high, text_low, logits, slope_high, slope_low, [first, second])
    for at, count in image_tiles(rows):
        place = pl.ds(at, count)
        early = at < known.shape[0]
        grad = known[place, :] if early else image_sum(o0, o1, o2, o3, at, count)
        grad = grad + image_sum(w0, w1, w2, w3, at, count)
        image_acc[place, :] = grad + image_sum(slope_high, slope_low, text_high, text_low, at, count)


def other_kernel(o0, o1, o2, o3, w0, w1, w2, w3, out):
    rows = out.shape[0]
    for at, count in image_tiles(rows):
        total = image_sum(o0, o1, o2, o3, rows + at, count) + image_sum(w0, w1, w2, w3, rows + at, count)
        out[pl.ds(at, count), :] = total


def image_kernel(images, known, received, out):
    out[...] = tangent_of(images[...], known[...] + received[...])


def add_kernel(left, right, out):
    out[...] = left[...] + right[...]


def text_kernel(first, texts, known, narrow, *refs):
    out, tangents, arrived = refs[-3:]
    step = 64
    copies = []
    for at in range(0, narrow.shape[0], step):
        here, there = pl.ds(at, step), pl.ds(first + at, step)
        grad = known[there, :] + narrow[here, :]
        tangents[here, :] = tangent_of(texts[there, :], grad)
        copies.append(pltpu.make_async_copy(tangents.at[here], out.at[there], arrived.at[at // step]))
        copies[-1].start()
    for copy in copies:
        copy.wait()


def cost(units):
    flops = int(units * 6 * 640 * 640 * 1152)
    return pl.CostEstimate(flops=flops, bytes_accessed=5_000_000 if units else 0, transcendentals=0)


IN_SMEM = pl.BlockSpec(memory_space=pltpu.SMEM)
IN_VMEM = pl.BlockSpec(memory_space=pltpu.VMEM)


def near(value):
    return pltpu.with_memory_space_constraint(value, pltpu.VMEM)


def vmem_call(kernel, outs, scratch, units, *arrays, numbers=(), aliases=None, limit=8, space=pltpu.VMEM):
    return pl.pallas_call(
        kernel,
        out_shape=[pltpu.VMEM(shape, kind) for shape, kind in outs],
        in_specs=[IN_SMEM] * len(numbers) + [pl.BlockSpec(memory_space=space)] * len(arrays),
        out_specs=[IN_VMEM] * len(outs),
        scratch_shapes=scratch,
        input_output_aliases=aliases or {},
        compiler_params=pltpu.CompilerParams(vmem_limit_bytes=limit * MIB),
        cost_estimate=cost(units),
    )(*numbers, *(pltpu.with_memory_space_constraint(a, space) for a in arrays))


def finish_images(images, known, received):
    rows, width = images.shape
    block = pl.BlockSpec((128, width), lambda i: (i, 0))
    return pl.pallas_call(
        image_kernel,
        grid=(rows // 128,),
        out_shape=jax.ShapeDtypeStruct(images.shape, F32),
        in_specs=[block] * 3,
        out_specs=block,
        compiler_params=pltpu.CompilerParams(vmem_limit_bytes=8 * MIB),
        cost_estimate=cost(0),
    )(images, known, received)


def finish_rows(first, texts, known, narrow, out=None):
    before = () if out is None else (out,)
    return pl.pallas_call(
        functools.partial(text_kernel, first),
        out_shape=jax.ShapeDtypeStruct(texts.shape, F32),
        in_specs=[IN_VMEM] * 3 + [pl.BlockSpec(memory_space=pl.ANY)] * len(before),
        out_specs=pl.BlockSpec(memory_space=pl.ANY),
        scratch_shapes=[pltpu.VMEM(narrow.shape, F32), pltpu.SemaphoreType.DMA((narrow.shape[0] // 64,))],
        input_output_aliases={3: 0} if before else {},
        compiler_params=pltpu.CompilerParams(vmem_limit_bytes=8 * MIB),
        cost_estimate=cost(0),
    )(near(texts), near(known), near(narrow), *before)


def on_device(images, texts, log_scale, bias):
    n = lax.axis_size("dp")
    rows, width = images.shape
    wide = [((i + 2) % n if i % 2 == 0 else (i - 2) % n, i) for i in range(n)]
    narrow = [((i - 2) % n if i % 2 == 0 else (i + 2) % n, i) for i in range(n)]
    swap = [(i ^ 1, i) for i in range(n)]
    wide_back = [(b, a) for a, b in wide]
    narrow_back = [(b, a) for a, b in narrow]
    block, half = ((rows, width), F32), ((rows, width), BF16)
    both = ((2 * rows, width), BF16)
    logits_wide, logits_narrow = pltpu.VMEM((rows, 2 * rows), F32), pltpu.VMEM((rows, rows), F32)
    slopes_wide, slopes_narrow = ((rows, 2 * rows), BF16), ((rows, rows), BF16)
    numbers = log_scale, bias

    wide_texts = lax.ppermute(texts, "dp", wide)
    others = lax.ppermute(images, "dp", swap)

    both_high, both_low, text_high, text_low, kept = vmem_call(
        prepare_kernel,
        [both, both, half, half, block],
        [pltpu.VMEM((rows, width), F32), pltpu.SemaphoreType.DMA((2 * rows // 128,))],
        0,
        images,
        texts,
        space=pltpu.HBM,
    )
    both_high, both_low, text_acc, image_acc, *own_slopes = vmem_call(
        own_kernel,
        [both, both, block, ((EARLY, width), F32), slopes_wide, slopes_wide],
        [logits_wide],
        5,
        others,
        text_high,
        text_low,
        both_high,
        both_low,
        numbers=numbers,
        aliases={5: 0, 6: 1},
    )

    text_acc, kept, both_high = lax.optimization_barrier((text_acc, kept, both_high))
    narrow_texts = lax.ppermute(kept, "dp", narrow)

    wide_grad, *wide_quad = vmem_call(
        wide_kernel,
        [block, slopes_wide, slopes_wide, half, half],
        [logits_wide],
        4,
        both_high,
        both_low,
        wide_texts,
        numbers=numbers,
    )
    wide_grad = lax.ppermute(wide_grad, "dp", wide_back)

    (other_acc,) = vmem_call(other_kernel, [block], [], 0, *own_slopes, text_high, text_low, *wide_quad)
    first, second, image_acc = vmem_call(
        narrow_kernel,
        [((FIRST, width), F32), ((rows - FIRST, width), F32), block],
        [pltpu.VMEM(*slopes_narrow)] * 2 + [pltpu.VMEM(*half)] * 2 + [logits_narrow],
        4,
        both_high,
        both_low,
        narrow_texts,
        image_acc,
        *own_slopes,
        text_high,
        text_low,
        *wide_quad,
        numbers=numbers,
        limit=10,
    )
    first = lax.ppermute(first, "dp", narrow_back)
    second = lax.ppermute(second, "dp", narrow_back)
    received = lax.ppermute(other_acc, "dp", swap)

    (known,) = vmem_call(add_kernel, [block], [], 6, text_acc, wide_grad, aliases={0: 0})
    image_acc, known = lax.optimization_barrier((image_acc, known))
    image_grad = finish_images(images, image_acc, received)
    image_grad, known = lax.optimization_barrier((image_grad, known))
    text_grad = finish_rows(0, kept, known, first)
    text_grad = finish_rows(FIRST, kept, known, second, text_grad)
    return (image_grad, text_grad)


def solution(mesh):
    in_specs = (P("dp", None), P("dp", None), P(), P())
    out_specs = (P("dp", None), P("dp", None))
    return jax.shard_map(
        on_device, mesh=mesh, in_specs=in_specs, out_specs=out_specs, check_vma=False
    )
```

```python
import functools

import jax
import jax.numpy as jnp
from jax import lax
from jax.experimental import pallas as pl
from jax.experimental.pallas import tpu as pltpu
from jax.sharding import PartitionSpec as P

EPSILON = 1e-06
TILE = 320
FIRST = 512
EARLY = 384
MIB = 1024 * 1024
F32 = jnp.float32
BF16 = jnp.bfloat16


def split(values):
    high = values.astype(BF16)
    return high, (values - high.astype(F32)).astype(BF16)


def inverse_norm(values):
    return lax.rsqrt(jnp.sum(values * values, axis=-1, keepdims=True) + EPSILON)


def product(a_high, a_low, b_high, b_low, a_dim, b_dim):
    dims = (((a_dim,), (b_dim,)), ((), ()))
    dot = functools.partial(lax.dot_general, dimension_numbers=dims, preferred_element_type=F32)
    return dot(a_high, b_high) + (dot(a_high, b_low) + dot(a_low, b_high))


def split_rows(source, high, low, at=0):
    step = 128

    @pl.loop(0, source.shape[0] // step)
    def _(i):
        values = source[pl.ds(pl.multiple_of(i * step, step), step), :]
        out = pl.ds(pl.multiple_of(at + i * step, step), step)
        high[out, :], low[out, :] = split(values * inverse_norm(values))


def logit_rows(at, count, image_high, image_low, text_high, text_low, logits):
    rows = pl.ds(at, count)
    logits[rows, :] = product(text_high[rows, :], text_low[rows, :], image_high[...], image_low[...], 1, 1)


def slope_rows(numbers, at, count, logits, slope_high, slope_low, diagonal=False):
    log_scale, bias = numbers
    columns = logits.shape[1]
    scale = jnp.exp(jnp.full((1, columns), log_scale[0], F32))
    gain = scale * (1.0 / logits.shape[0])
    step = 64

    @pl.loop(0, count // step)
    def _(k):
        start = pl.multiple_of(at + k * step, step)
        rows = pl.ds(start, step)
        x = scale * logits[rows, :] + bias[0]
        half = columns // 2
        if diagonal:
            own = x[:, :half]
            j = lax.broadcasted_iota(jnp.int32, own.shape, 0) + start
            i = lax.broadcasted_iota(jnp.int32, own.shape, 1)
            sign = jnp.where(i == j, -1.0, 1.0)
            slopes = (gain[:, :half] * sign) / (1.0 + jnp.exp(-sign * own))
            slope_high[rows, pl.ds(0, half)], slope_low[rows, pl.ds(0, half)] = split(slopes)
            rest = pl.ds(half, half)
            slopes = gain[:, half:] / (1.0 + jnp.exp(-x[:, half:]))
            slope_high[rows, rest], slope_low[rows, rest] = split(slopes)
        else:
            slope_high[rows, :], slope_low[rows, :] = split(gain / (1.0 + jnp.exp(-x)))


def text_sum(at, count, slope_high, slope_low, image_high, image_low):
    rows = pl.ds(at, count)
    return product(slope_high[rows, :], slope_low[rows, :], image_high[...], image_low[...], 1, 0)


def text_side(numbers, image_high, image_low, text_high, text_low, logits, slope_high, slope_low, grads, diagonal=False):
    rows = text_high.shape[0]
    for at in range(0, rows, TILE):
        logit_rows(at, TILE, image_high, image_low, text_high, text_low, logits)
    slope_rows(numbers, 0, rows, logits, slope_high, slope_low, diagonal)
    first = 0
    for grad in grads:
        count = grad.shape[0]
        for at in range(0, count, TILE if count == rows else count):
            size = min(TILE, count) if count == rows else count
            grad[pl.ds(at, size), :] = text_sum(first + at, size, slope_high, slope_low, image_high, image_low)
        first += count


def image_tiles(rows):
    return [(at, min(256, rows - at)) for at in range(0, rows, 256)]


def image_sum(slope_high, slope_low, text_high, text_low, at, count):
    columns = pl.ds(at, count)
    return product(slope_high[:, columns], slope_low[:, columns], text_high[...], text_low[...], 0, 0)


def tangent_of(values, grad):
    inverse = inverse_norm(values)
    unit = values * inverse
    return (grad - unit * jnp.sum(unit * grad, axis=-1, keepdims=True)) * inverse


def prepare_kernel(images, texts, both_high, both_low, text_high, text_low, kept, own, arrived):
    step = 128
    parts = images.shape[0] // step
    copies = []
    for k in range(parts):
        rows = pl.ds(k * step, step)
        copies.append(pltpu.make_async_copy(images.at[rows], own.at[rows], arrived.at[k]))
    for k in range(parts):
        rows = pl.ds(k * step, step)
        copies.append(pltpu.make_async_copy(texts.at[rows], kept.at[rows], arrived.at[parts + k]))
    for copy in copies:
        copy.start()
    for k, copy in enumerate(copies):
        copy.wait()
        source, high, low = (own, both_high, both_low) if k < parts else (kept, text_high, text_low)
        rows = pl.ds(k % parts * step, step)
        values = source[rows, :]
        high[rows, :], low[rows, :] = split(values * inverse_norm(values))


def own_kernel(log_scale, bias, others, text_high, text_low, high_in, low_in, both_high, both_low, text_acc, image_acc, slope_high, slope_low, logits):
    rows = others.shape[0]
    split_rows(others, both_high, both_low, rows)
    numbers = log_scale, bias
    text_side(numbers, both_high, both_low, text_high, text_low, logits, slope_high, slope_low, [text_acc], True)
    for at, count in image_tiles(image_acc.shape[0]):
        image_acc[pl.ds(at, count), :] = image_sum(slope_high, slope_low, text_high, text_low, at, count)


def wide_kernel(log_scale, bias, image_high, image_low, texts, grad, slope_high, slope_low, text_high, text_low, logits):
    split_rows(texts, text_high, text_low)
    numbers = log_scale, bias
    text_side(numbers, image_high, image_low, text_high, text_low, logits, slope_high, slope_low, [grad])


def narrow_kernel(log_scale, bias, both_high, both_low, texts, known, o0, o1, o2, o3, w0, w1, w2, w3, first, second, image_acc, slope_high, slope_low, text_high, text_low, logits):
    rows = texts.shape[0]
    split_rows(texts, text_high, text_low)
    image_high, image_low = both_high.at[pl.ds(0, rows)], both_low.at[pl.ds(0, rows)]
    numbers = log_scale, bias
    text_side(numbers, image_high, image_low, text_high, text_low, logits, slope_high, slope_low, [first, second])
    early_rows = known.shape[0]
    later = [(early_rows + at, count) for at, count in image_tiles(rows - early_rows)]
    for at, count in image_tiles(early_rows) + later:
        place = pl.ds(at, count)
        early = at < early_rows
        grad = known[place, :] if early else image_sum(o0, o1, o2, o3, at, count)
        grad = grad + image_sum(w0, w1, w2, w3, at, count)
        image_acc[place, :] = grad + image_sum(slope_high, slope_low, text_high, text_low, at, count)


def other_kernel(o0, o1, o2, o3, w0, w1, w2, w3, out):
    rows = out.shape[0]
    for at, count in image_tiles(rows):
        total = image_sum(o0, o1, o2, o3, rows + at, count) + image_sum(w0, w1, w2, w3, rows + at, count)
        out[pl.ds(at, count), :] = total


def image_kernel(images, known, received, out):
    out[...] = tangent_of(images[...], known[...] + received[...])


def add_kernel(left, right, out):
    out[...] = left[...] + right[...]


def text_kernel(first, texts, known, narrow, *refs):
    out, tangents, arrived = refs[-3:]
    step = 64
    copies = []
    for at in range(0, narrow.shape[0], step):
        here, there = pl.ds(at, step), pl.ds(first + at, step)
        grad = known[there, :] + narrow[here, :]
        tangents[here, :] = tangent_of(texts[there, :], grad)
        copies.append(pltpu.make_async_copy(tangents.at[here], out.at[there], arrived.at[at // step]))
        copies[-1].start()
    for copy in copies:
        copy.wait()


def cost(units):
    flops = int(units * 6 * 640 * 640 * 1152)
    return pl.CostEstimate(flops=flops, bytes_accessed=5_000_000 if units else 0, transcendentals=0)


IN_SMEM = pl.BlockSpec(memory_space=pltpu.SMEM)
IN_VMEM = pl.BlockSpec(memory_space=pltpu.VMEM)


def near(value):
    return pltpu.with_memory_space_constraint(value, pltpu.VMEM)


def vmem_call(kernel, outs, scratch, units, *arrays, numbers=(), aliases=None, limit=8, space=pltpu.VMEM):
    return pl.pallas_call(
        kernel,
        out_shape=[pltpu.VMEM(shape, kind) for shape, kind in outs],
        in_specs=[IN_SMEM] * len(numbers) + [pl.BlockSpec(memory_space=space)] * len(arrays),
        out_specs=[IN_VMEM] * len(outs),
        scratch_shapes=scratch,
        input_output_aliases=aliases or {},
        compiler_params=pltpu.CompilerParams(vmem_limit_bytes=limit * MIB),
        cost_estimate=cost(units),
    )(*numbers, *(pltpu.with_memory_space_constraint(a, space) for a in arrays))


def finish_images(images, known, received):
    rows, width = images.shape
    block = pl.BlockSpec((128, width), lambda i: (i, 0))
    return pl.pallas_call(
        image_kernel,
        grid=(rows // 128,),
        out_shape=jax.ShapeDtypeStruct(images.shape, F32),
        in_specs=[block] * 3,
        out_specs=block,
        compiler_params=pltpu.CompilerParams(vmem_limit_bytes=8 * MIB),
        cost_estimate=cost(0),
    )(images, known, received)


def finish_rows(first, texts, known, narrow, out=None):
    before = () if out is None else (out,)
    return pl.pallas_call(
        functools.partial(text_kernel, first),
        out_shape=jax.ShapeDtypeStruct(texts.shape, F32),
        in_specs=[IN_VMEM] * 3 + [pl.BlockSpec(memory_space=pl.ANY)] * len(before),
        out_specs=pl.BlockSpec(memory_space=pl.ANY),
        scratch_shapes=[pltpu.VMEM(narrow.shape, F32), pltpu.SemaphoreType.DMA((narrow.shape[0] // 64,))],
        input_output_aliases={3: 0} if before else {},
        compiler_params=pltpu.CompilerParams(vmem_limit_bytes=8 * MIB),
        cost_estimate=cost(0),
    )(near(texts), near(known), near(narrow), *before)


def on_device(images, texts, log_scale, bias):
    n = lax.axis_size("dp")
    rows, width = images.shape
    wide = [((i + 2) % n if i % 2 == 0 else (i - 2) % n, i) for i in range(n)]
    narrow = [((i - 2) % n if i % 2 == 0 else (i + 2) % n, i) for i in range(n)]
    swap = [(i ^ 1, i) for i in range(n)]
    wide_back = [(b, a) for a, b in wide]
    narrow_back = [(b, a) for a, b in narrow]
    block, half = ((rows, width), F32), ((rows, width), BF16)
    both = ((2 * rows, width), BF16)
    logits_wide, logits_narrow = pltpu.VMEM((rows, 2 * rows), F32), pltpu.VMEM((rows, rows), F32)
    slopes_wide, slopes_narrow = ((rows, 2 * rows), BF16), ((rows, rows), BF16)
    numbers = log_scale, bias

    wide_texts = lax.ppermute(texts, "dp", wide)
    others = lax.ppermute(images, "dp", swap)

    both_high, both_low, text_high, text_low, kept = vmem_call(
        prepare_kernel,
        [both, both, half, half, block],
        [pltpu.VMEM((rows, width), F32), pltpu.SemaphoreType.DMA((2 * rows // 128,))],
        0,
        images,
        texts,
        space=pltpu.HBM,
    )
    both_high, both_low, text_acc, image_acc, *own_slopes = vmem_call(
        own_kernel,
        [both, both, block, ((EARLY, width), F32), slopes_wide, slopes_wide],
        [logits_wide],
        5,
        others,
        text_high,
        text_low,
        both_high,
        both_low,
        numbers=numbers,
        aliases={5: 0, 6: 1},
    )

    text_acc, kept, both_high = lax.optimization_barrier((text_acc, kept, both_high))
    narrow_texts = lax.ppermute(kept, "dp", narrow)

    wide_grad, *wide_quad = vmem_call(
        wide_kernel,
        [block, slopes_wide, slopes_wide, half, half],
        [logits_wide],
        4,
        both_high,
        both_low,
        wide_texts,
        numbers=numbers,
    )
    wide_grad = lax.ppermute(wide_grad, "dp", wide_back)

    (other_acc,) = vmem_call(other_kernel, [block], [], 0, *own_slopes, text_high, text_low, *wide_quad)
    first, second, image_acc = vmem_call(
        narrow_kernel,
        [((FIRST, width), F32), ((rows - FIRST, width), F32), block],
        [pltpu.VMEM(*slopes_narrow)] * 2 + [pltpu.VMEM(*half)] * 2 + [logits_narrow],
        4,
        both_high,
        both_low,
        narrow_texts,
        image_acc,
        *own_slopes,
        text_high,
        text_low,
        *wide_quad,
        numbers=numbers,
        limit=10,
    )
    first = lax.ppermute(first, "dp", narrow_back)
    second = lax.ppermute(second, "dp", narrow_back)
    received = lax.ppermute(other_acc, "dp", swap)

    (known,) = vmem_call(add_kernel, [block], [], 6, text_acc, wide_grad, aliases={0: 0})
    image_acc, known = lax.optimization_barrier((image_acc, known))
    image_grad = finish_images(images, image_acc, received)
    image_grad, known = lax.optimization_barrier((image_grad, known))
    text_grad = finish_rows(0, kept, known, first)
    text_grad = finish_rows(FIRST, kept, known, second, text_grad)
    return (image_grad, text_grad)


def solution(mesh):
    in_specs = (P("dp", None), P("dp", None), P(), P())
    out_specs = (P("dp", None), P("dp", None))
    return jax.shard_map(
        on_device, mesh=mesh, in_specs=in_specs, out_specs=out_specs, check_vma=False
    )
```

```python
import functools

import jax
import jax.numpy as jnp
from jax import lax
from jax.experimental import pallas as pl
from jax.experimental.pallas import tpu as pltpu
from jax.sharding import PartitionSpec as P

EPSILON = 1e-06
TILE = 320
FIRST = 512
EARLY = 128
MIB = 1024 * 1024
F32 = jnp.float32
BF16 = jnp.bfloat16


def split(values):
    high = values.astype(BF16)
    return high, (values - high.astype(F32)).astype(BF16)


def inverse_norm(values):
    return lax.rsqrt(jnp.sum(values * values, axis=-1, keepdims=True) + EPSILON)


def product(a_high, a_low, b_high, b_low, a_dim, b_dim):
    dims = (((a_dim,), (b_dim,)), ((), ()))
    dot = functools.partial(lax.dot_general, dimension_numbers=dims, preferred_element_type=F32)
    return dot(a_high, b_high) + (dot(a_high, b_low) + dot(a_low, b_high))


def split_rows(source, high, low, at=0):
    step = 128

    @pl.loop(0, source.shape[0] // step)
    def _(i):
        values = source[pl.ds(pl.multiple_of(i * step, step), step), :]
        out = pl.ds(pl.multiple_of(at + i * step, step), step)
        high[out, :], low[out, :] = split(values * inverse_norm(values))


def logit_rows(at, count, image_high, image_low, text_high, text_low, logits):
    rows = pl.ds(at, count)
    logits[rows, :] = product(text_high[rows, :], text_low[rows, :], image_high[...], image_low[...], 1, 1)


def slope_rows(numbers, at, count, logits, slope_high, slope_low, diagonal=False):
    log_scale, bias = numbers
    columns = logits.shape[1]
    scale = jnp.exp(jnp.full((1, columns), log_scale[0], F32))
    gain = scale * (1.0 / logits.shape[0])
    step = 64

    @pl.loop(0, count // step)
    def _(k):
        start = pl.multiple_of(at + k * step, step)
        rows = pl.ds(start, step)
        x = scale * logits[rows, :] + bias[0]
        half = columns // 2
        if diagonal:
            own = x[:, :half]
            j = lax.broadcasted_iota(jnp.int32, own.shape, 0) + start
            i = lax.broadcasted_iota(jnp.int32, own.shape, 1)
            sign = jnp.where(i == j, -1.0, 1.0)
            slopes = (gain[:, :half] * sign) / (1.0 + jnp.exp(-sign * own))
            slope_high[rows, pl.ds(0, half)], slope_low[rows, pl.ds(0, half)] = split(slopes)
            rest = pl.ds(half, half)
            slopes = gain[:, half:] / (1.0 + jnp.exp(-x[:, half:]))
            slope_high[rows, rest], slope_low[rows, rest] = split(slopes)
        else:
            slope_high[rows, :], slope_low[rows, :] = split(gain / (1.0 + jnp.exp(-x)))


def text_sum(at, count, slope_high, slope_low, image_high, image_low):
    rows = pl.ds(at, count)
    return product(slope_high[rows, :], slope_low[rows, :], image_high[...], image_low[...], 1, 0)


def text_side(numbers, image_high, image_low, text_high, text_low, logits, slope_high, slope_low, grads, diagonal=False):
    rows = text_high.shape[0]
    for at in range(0, rows, TILE):
        logit_rows(at, TILE, image_high, image_low, text_high, text_low, logits)
    slope_rows(numbers, 0, rows, logits, slope_high, slope_low, diagonal)
    first = 0
    for grad in grads:
        count = grad.shape[0]
        for at in range(0, count, TILE if count == rows else count):
            size = min(TILE, count) if count == rows else count
            grad[pl.ds(at, size), :] = text_sum(first + at, size, slope_high, slope_low, image_high, image_low)
        first += count


def image_tiles(rows):
    return [(at, min(256, rows - at)) for at in range(0, rows, 256)]


def image_sum(slope_high, slope_low, text_high, text_low, at, count):
    columns = pl.ds(at, count)
    return product(slope_high[:, columns], slope_low[:, columns], text_high[...], text_low[...], 0, 0)


def tangent_of(values, grad):
    inverse = inverse_norm(values)
    unit = values * inverse
    return (grad - unit * jnp.sum(unit * grad, axis=-1, keepdims=True)) * inverse


def prepare_kernel(images, texts, both_high, both_low, text_high, text_low, kept, own, arrived):
    step = 128
    parts = images.shape[0] // step
    copies = []
    for k in range(parts):
        rows = pl.ds(k * step, step)
        copies.append(pltpu.make_async_copy(images.at[rows], own.at[rows], arrived.at[k]))
    for k in range(parts):
        rows = pl.ds(k * step, step)
        copies.append(pltpu.make_async_copy(texts.at[rows], kept.at[rows], arrived.at[parts + k]))
    for copy in copies:
        copy.start()
    for k, copy in enumerate(copies):
        copy.wait()
        source, high, low = (own, both_high, both_low) if k < parts else (kept, text_high, text_low)
        rows = pl.ds(k % parts * step, step)
        values = source[rows, :]
        high[rows, :], low[rows, :] = split(values * inverse_norm(values))


def own_kernel(log_scale, bias, others, text_high, text_low, high_in, low_in, both_high, both_low, text_acc, image_acc, slope_high, slope_low, logits):
    rows = others.shape[0]
    split_rows(others, both_high, both_low, rows)
    numbers = log_scale, bias
    text_side(numbers, both_high, both_low, text_high, text_low, logits, slope_high, slope_low, [text_acc], True)
    for at, count in image_tiles(image_acc.shape[0]):
        image_acc[pl.ds(at, count), :] = image_sum(slope_high, slope_low, text_high, text_low, at, count)


def wide_kernel(log_scale, bias, image_high, image_low, texts, grad, slope_high, slope_low, text_high, text_low, logits):
    split_rows(texts, text_high, text_low)
    numbers = log_scale, bias
    text_side(numbers, image_high, image_low, text_high, text_low, logits, slope_high, slope_low, [grad])


def narrow_kernel(log_scale, bias, both_high, both_low, texts, known, o0, o1, o2, o3, w0, w1, w2, w3, first, second, image_acc, slope_high, slope_low, text_high, text_low, logits):
    rows = texts.shape[0]
    split_rows(texts, text_high, text_low)
    image_high, image_low = both_high.at[pl.ds(0, rows)], both_low.at[pl.ds(0, rows)]
    numbers = log_scale, bias
    text_side(numbers, image_high, image_low, text_high, text_low, logits, slope_high, slope_low, [first, second])
    early_rows = known.shape[0]
    later = [(early_rows + at, count) for at, count in image_tiles(rows - early_rows)]
    for at, count in image_tiles(early_rows) + later:
        place = pl.ds(at, count)
        early = at < early_rows
        grad = known[place, :] if early else image_sum(o0, o1, o2, o3, at, count)
        grad = grad + image_sum(w0, w1, w2, w3, at, count)
        image_acc[place, :] = grad + image_sum(slope_high, slope_low, text_high, text_low, at, count)


def other_kernel(o0, o1, o2, o3, w0, w1, w2, w3, out):
    rows = out.shape[0]
    for at, count in image_tiles(rows):
        total = image_sum(o0, o1, o2, o3, rows + at, count) + image_sum(w0, w1, w2, w3, rows + at, count)
        out[pl.ds(at, count), :] = total


def image_kernel(images, known, received, out):
    out[...] = tangent_of(images[...], known[...] + received[...])


def add_kernel(left, right, out):
    out[...] = left[...] + right[...]


def text_kernel(first, texts, known, narrow, *refs):
    out, tangents, arrived = refs[-3:]
    step = 64
    copies = []
    for at in range(0, narrow.shape[0], step):
        here, there = pl.ds(at, step), pl.ds(first + at, step)
        grad = known[there, :] + narrow[here, :]
        tangents[here, :] = tangent_of(texts[there, :], grad)
        copies.append(pltpu.make_async_copy(tangents.at[here], out.at[there], arrived.at[at // step]))
        copies[-1].start()
    for copy in copies:
        copy.wait()


def cost(units):
    flops = int(units * 6 * 640 * 640 * 1152)
    return pl.CostEstimate(flops=flops, bytes_accessed=5_000_000 if units else 0, transcendentals=0)


IN_SMEM = pl.BlockSpec(memory_space=pltpu.SMEM)
IN_VMEM = pl.BlockSpec(memory_space=pltpu.VMEM)


def near(value):
    return pltpu.with_memory_space_constraint(value, pltpu.VMEM)


def vmem_call(kernel, outs, scratch, units, *arrays, numbers=(), aliases=None, limit=8, space=pltpu.VMEM):
    return pl.pallas_call(
        kernel,
        out_shape=[pltpu.VMEM(shape, kind) for shape, kind in outs],
        in_specs=[IN_SMEM] * len(numbers) + [pl.BlockSpec(memory_space=space)] * len(arrays),
        out_specs=[IN_VMEM] * len(outs),
        scratch_shapes=scratch,
        input_output_aliases=aliases or {},
        compiler_params=pltpu.CompilerParams(vmem_limit_bytes=limit * MIB),
        cost_estimate=cost(units),
    )(*numbers, *(pltpu.with_memory_space_constraint(a, space) for a in arrays))


def finish_images(images, known, received):
    rows, width = images.shape
    block = pl.BlockSpec((128, width), lambda i: (i, 0))
    return pl.pallas_call(
        image_kernel,
        grid=(rows // 128,),
        out_shape=jax.ShapeDtypeStruct(images.shape, F32),
        in_specs=[block] * 3,
        out_specs=block,
        compiler_params=pltpu.CompilerParams(vmem_limit_bytes=8 * MIB),
        cost_estimate=cost(0),
    )(images, known, received)


def finish_rows(first, texts, known, narrow, out=None):
    before = () if out is None else (out,)
    return pl.pallas_call(
        functools.partial(text_kernel, first),
        out_shape=jax.ShapeDtypeStruct(texts.shape, F32),
        in_specs=[IN_VMEM] * 3 + [pl.BlockSpec(memory_space=pl.ANY)] * len(before),
        out_specs=pl.BlockSpec(memory_space=pl.ANY),
        scratch_shapes=[pltpu.VMEM(narrow.shape, F32), pltpu.SemaphoreType.DMA((narrow.shape[0] // 64,))],
        input_output_aliases={3: 0} if before else {},
        compiler_params=pltpu.CompilerParams(vmem_limit_bytes=8 * MIB),
        cost_estimate=cost(0),
    )(near(texts), near(known), near(narrow), *before)


def on_device(images, texts, log_scale, bias):
    n = lax.axis_size("dp")
    rows, width = images.shape
    wide = [((i + 2) % n if i % 2 == 0 else (i - 2) % n, i) for i in range(n)]
    narrow = [((i - 2) % n if i % 2 == 0 else (i + 2) % n, i) for i in range(n)]
    swap = [(i ^ 1, i) for i in range(n)]
    wide_back = [(b, a) for a, b in wide]
    narrow_back = [(b, a) for a, b in narrow]
    block, half = ((rows, width), F32), ((rows, width), BF16)
    both = ((2 * rows, width), BF16)
    logits_wide, logits_narrow = pltpu.VMEM((rows, 2 * rows), F32), pltpu.VMEM((rows, rows), F32)
    slopes_wide, slopes_narrow = ((rows, 2 * rows), BF16), ((rows, rows), BF16)
    numbers = log_scale, bias

    wide_texts = lax.ppermute(texts, "dp", wide)
    others = lax.ppermute(images, "dp", swap)

    both_high, both_low, text_high, text_low, kept = vmem_call(
        prepare_kernel,
        [both, both, half, half, block],
        [pltpu.VMEM((rows, width), F32), pltpu.SemaphoreType.DMA((2 * rows // 128,))],
        0,
        images,
        texts,
        space=pltpu.HBM,
    )
    both_high, both_low, text_acc, image_acc, *own_slopes = vmem_call(
        own_kernel,
        [both, both, block, ((EARLY, width), F32), slopes_wide, slopes_wide],
        [logits_wide],
        5,
        others,
        text_high,
        text_low,
        both_high,
        both_low,
        numbers=numbers,
        aliases={5: 0, 6: 1},
    )

    text_acc, kept, both_high = lax.optimization_barrier((text_acc, kept, both_high))
    narrow_texts = lax.ppermute(kept, "dp", narrow)

    wide_grad, *wide_quad = vmem_call(
        wide_kernel,
        [block, slopes_wide, slopes_wide, half, half],
        [logits_wide],
        4,
        both_high,
        both_low,
        wide_texts,
        numbers=numbers,
    )
    wide_grad = lax.ppermute(wide_grad, "dp", wide_back)

    (other_acc,) = vmem_call(other_kernel, [block], [], 0, *own_slopes, text_high, text_low, *wide_quad)
    first, second, image_acc = vmem_call(
        narrow_kernel,
        [((FIRST, width), F32), ((rows - FIRST, width), F32), block],
        [pltpu.VMEM(*slopes_narrow)] * 2 + [pltpu.VMEM(*half)] * 2 + [logits_narrow],
        4,
        both_high,
        both_low,
        narrow_texts,
        image_acc,
        *own_slopes,
        text_high,
        text_low,
        *wide_quad,
        numbers=numbers,
        limit=12,
    )
    first = lax.ppermute(first, "dp", narrow_back)
    second = lax.ppermute(second, "dp", narrow_back)
    received = lax.ppermute(other_acc, "dp", swap)

    (known,) = vmem_call(add_kernel, [block], [], 6, text_acc, wide_grad, aliases={0: 0})
    image_acc, known = lax.optimization_barrier((image_acc, known))
    image_grad = finish_images(images, image_acc, received)
    image_grad, known = lax.optimization_barrier((image_grad, known))
    text_grad = finish_rows(0, kept, known, first)
    text_grad = finish_rows(FIRST, kept, known, second, text_grad)
    return (image_grad, text_grad)


def solution(mesh):
    in_specs = (P("dp", None), P("dp", None), P(), P())
    out_specs = (P("dp", None), P("dp", None))
    return jax.shard_map(
        on_device, mesh=mesh, in_specs=in_specs, out_specs=out_specs, check_vma=False
    )
```
